32 devices in a mesh: row: 2 (over core), col: 4 (over y, x), depth: 4 (over z).
Axes of the slice: x: 2, y: 2, z: 4, core: 2. Of those that a mesh axis runs over, the one named last changes fastest.
Arguments:
- tokens: bfloat16 [128, 12288], P(('col', 'depth'), 'row'), may hold values from -6 to 6
- cotangent: bfloat16 [128, 12288], P(('col', 'depth'), 'row'), may hold values from -0.375 to 0.375
- w_in: bfloat16 [12288, 24576], P('row', ('col', 'depth')), may hold values from -0.0546875 to 0.0546875
- b_in: float32 [24576], P('col'), may hold values from -4 to 4
- w_out: bfloat16 [24576, 12288], P('col', ('row', 'depth')), may hold values from -0.0390625 to 0.0390625
Outputs:
- input_grad: bfloat16 [128, 12288], P(('col', 'depth'), 'row')
- w_in_grad: bfloat16 [12288, 24576], P('row', ('col', 'depth'))
- b_in_grad: float32 [24576], P(('col', 'depth'))
- w_out_grad: bfloat16 [24576, 12288], P('col', ('row', 'depth'))
The draws below stay inside these ranges and needn't reach their ends.
All inputs are finite; a program needn't handle non-finite values.
Results may differ from the reference program's by a relative error of at most 0.0065.
Values may be sent and summed in bfloat16 or wider, within the bound.
A program may use at most 320 MiB of HBM per device.

```python
import jax
import jax.numpy as jnp

D = 12288
H = 24576
TOKENS = 128


def levels(key, extent, cuts, low, largest):
    def one(axis_at, blocks):
        steps = jax.random.uniform(jax.random.fold_in(jax.random.fold_in(key, 6), axis_at), (blocks,), jnp.float32, low / len(cuts), largest / len(cuts))
        return jnp.repeat(jnp.exp(steps), extent[axis_at] // blocks).reshape((-1,) + (1,) * (len(extent) - axis_at - 1))

    gain = one(*cuts[0])
    for cut in cuts[1:]:
        gain = gain * one(*cut)
    return gain


def normal_values(own_key, extent, deviation, limit, split=(), dtype=jnp.bfloat16):
    loudness = levels(own_key, extent, split, -0.22, 0.18) if split else 1.0
    values = jax.random.normal(own_key, extent, jnp.float32) * deviation * loudness
    return jnp.minimum(jnp.maximum(values, -limit), limit).astype(dtype)


def setup_inputs(seed: int = 0) -> dict:
    streams_of = jax.random.split(jax.random.key(seed), 6)
    tokens = normal_values(streams_of[0], (TOKENS, D), 1.0, 6.0, ((0, 16), (1, 2)))
    cotangent = normal_values(streams_of[1], (TOKENS, D), 0.0625, 0.375, ((0, 16), (1, 2)))
    w_in = normal_values(streams_of[2], (D, H), D ** -0.5, 0.0546875, ((0, 2), (1, 16)))
    b_in = normal_values(streams_of[3], (H,), 1.0, 4.0, ((0, 4),), jnp.float32)
    w_out = normal_values(streams_of[4], (H, D), H ** -0.5, 0.0390625, ((0, 4), (1, 8)))
    return {"tokens": tokens, "cotangent": cotangent, "w_in": w_in, "b_in": b_in, "w_out": w_out}


coef = 0.7978845608


def gelu_pair(pre):
    inner = coef * (pre + 0.044715 * pre * pre * pre)
    tanh_v = jnp.tanh(inner)
    act = 0.5 * pre * (1.0 + tanh_v)
    slope = 0.5 * (1.0 + tanh_v) + 0.5 * pre * (1.0 - tanh_v * tanh_v) * coef * (1.0 + 0.134145 * pre * pre)
    return act, slope


def reference(tokens, cotangent, w_in, b_in, w_out):
    pre = jnp.dot(tokens, w_in, preferred_element_type=jnp.float32) + b_in
    act_f, slope = gelu_pair(pre)
    act = act_f.astype(jnp.bfloat16)
    back = jnp.dot(cotangent, w_out.T, preferred_element_type=jnp.float32)
    grad_pre = (back * slope).astype(jnp.bfloat16)
    w_out_grad = jnp.dot(act.T, cotangent, preferred_element_type=jnp.float32).astype(jnp.bfloat16)
    w_in_grad = jnp.dot(tokens.T, grad_pre, preferred_element_type=jnp.float32).astype(jnp.bfloat16)
    b_in_grad = jnp.sum(grad_pre.astype(jnp.float32), axis=0)
    input_grad = jnp.dot(grad_pre, w_in.T, preferred_element_type=jnp.float32).astype(jnp.bfloat16)
    return input_grad, w_in_grad, b_in_grad, w_out_grad
```

```python
import jax
import jax.numpy as jnp
from jax import lax
from jax.sharding import PartitionSpec as P

coef = 0.7978845608


def gelu_pair(pre):
    inner = coef * (pre + 0.044715 * pre * pre * pre)
    tanh_v = jnp.tanh(inner)
    act = 0.5 * pre * (1.0 + tanh_v)
    slope = 0.5 * (1.0 + tanh_v) + 0.5 * pre * (1.0 - tanh_v * tanh_v) * coef * (
        1.0 + 0.134145 * pre * pre
    )
    return (act, slope)


def against(left, right):
    return lax.dot_general(
        left, right, (((1,), (1,)), ((), ())), preferred_element_type=jnp.float32
    )


def shards(tokens, cotangent, w_in, b_in, w_out):
    depth_at = lax.axis_index("depth")
    quarter_h = w_in.shape[1]
    every_x = lax.all_gather(tokens, ("col", "depth"), axis=0, tiled=True)
    part_g = lax.all_to_all(cotangent, "depth", split_axis=1, concat_axis=0, tiled=True)
    quarter_g = lax.all_gather(part_g, "col", axis=0, tiled=True)
    back_part = against(quarter_g, w_out)
    back_half = lax.psum_scatter(back_part, "row", scatter_dimension=0, tiled=True)
    back_rows = lax.psum_scatter(back_half, "depth", scatter_dimension=1, tiled=True)
    pre_part = jnp.dot(every_x, w_in, preferred_element_type=jnp.float32)
    pre_rows = lax.psum_scatter(pre_part, "row", scatter_dimension=0, tiled=True)
    pre_rows = pre_rows + lax.dynamic_slice_in_dim(b_in, depth_at * quarter_h, quarter_h, 0)
    act_f, slope = gelu_pair(pre_rows)
    act = act_f.astype(jnp.bfloat16)
    grad_pre = (back_rows * slope).astype(jnp.bfloat16)
    quarter_grad = lax.all_gather(grad_pre, "row", axis=0, tiled=True)
    input_part = against(quarter_grad, w_in)
    input_grad = lax.psum_scatter(
        input_part, ("col", "depth"), scatter_dimension=0, tiled=True
    ).astype(jnp.bfloat16)
    act_half = lax.all_gather(act, "depth", axis=1, tiled=True)
    all_act = lax.all_gather(act_half, "row", axis=0, tiled=True)
    over_tokens = (((0,), (0,)), ((), ()))
    w_in_sum = lax.dot_general(
        every_x, quarter_grad, over_tokens, preferred_element_type=jnp.float32
    )
    w_out_sum = lax.dot_general(
        all_act, quarter_g, over_tokens, preferred_element_type=jnp.float32
    )
    b_in_grad = jnp.sum(quarter_grad.astype(jnp.float32), axis=0)
    return (input_grad, w_in_sum.astype(jnp.bfloat16), b_in_grad, w_out_sum.astype(jnp.bfloat16))


def solution(mesh):
    return jax.shard_map(
        shards,
        mesh=mesh,
        in_specs=(
            P(("col", "depth"), "row"),
            P(("col", "depth"), "row"),
            P("row", ("col", "depth")),
            P("col"),
            P("col", ("row", "depth")),
        ),
        out_specs=(
            P(("col", "depth"), "row"),
            P("row", ("col", "depth")),
            P(("col", "depth")),
            P("col", ("row", "depth")),
        ),
        check_vma=False,
    )
```

```python
import functools

import jax
import jax.numpy as jnp
from jax import lax
from jax.experimental import pallas as pl
from jax.experimental.pallas import tpu as pltpu
from jax.sharding import PartitionSpec as P

coef = 0.7978845608
MESH = pl.DeviceIdType.MESH
F32 = jnp.float32
BF16 = jnp.bfloat16
N_CHUNK = 4


def gelu_pair(pre):
    inner = coef * (pre + 0.044715 * pre * pre * pre)
    tanh_v = jnp.tanh(inner)
    act = 0.5 * pre * (1.0 + tanh_v)
    slope = 0.5 * (1.0 + tanh_v) + 0.5 * pre * (1.0 - tanh_v * tanh_v) * coef * (
        1.0 + 0.134145 * pre * pre
    )
    return (act, slope)


def against(left, right):
    return lax.dot_general(left, right, (((1,), (1,)), ((), ())), preferred_element_type=F32)


def over_tokens(left, right):
    return lax.dot_general(left, right, (((0,), (0,)), ((), ())), preferred_element_type=F32)


def block_of(size, largest=512):
    for block in (512, 384, 256, 128):
        if block <= largest and size % block == 0:
            return block
    return size


def cols_at(i, block):
    return pl.ds(pl.multiple_of(i * block, block), block)


def exchange_kernel(
    R, C, Z,
    tok_ref, cot_ref, w_in_hbm, b_ref, w_out_hbm,
    x_out, g_out, grad_out, act_out, bias_out, in_out,
    w_in_v, w_out_v, x_all, g_all, pre_part, pre_recv, back_part, back_recv,
    back_send, back_depth, act_all, grad_all, col_send, col_recv, dep_send, dep_recv,
    w_sem, x_s, x_r, g_s, g_r, pre_s, pre_r, br_s, br_r, bd_s, bd_r,
    act_s, act_r, grad_s, grad_r, col_s, col_r, dep_s, dep_r,
):
    row, col, dep = lax.axis_index("row"), lax.axis_index("col"), lax.axis_index("depth")
    size = {"row": R, "col": C, "depth": Z}
    here = {"row": row, "col": col, "depth": dep}

    def peer(axis, off):
        return lax.rem(here[axis] + off, size[axis])

    def source(axis, off):
        return lax.rem(here[axis] + size[axis] - off, size[axis])

    pending = []

    def send(axis, off, src, dst, s, r):
        copy = pltpu.make_async_remote_copy(
            src_ref=src, dst_ref=dst, send_sem=s, recv_sem=r,
            device_id={axis: peer(axis, off)}, device_id_type=MESH,
        )
        copy.start()
        pending.append(copy)
        return copy

    load_out = pltpu.make_async_copy(w_out_hbm, w_out_v, w_sem.at[0])
    load_in = pltpu.make_async_copy(w_in_hbm, w_in_v, w_sem.at[1])
    load_out.start()
    load_in.start()

    barrier = pltpu.get_barrier_semaphore()
    for axis in ("row", "col", "depth"):
        for off in range(1, size[axis]):
            pl.semaphore_signal(
                barrier, inc=1, device_id={axis: peer(axis, off)}, device_id_type=MESH
            )
    pl.semaphore_wait(barrier, R + C + Z - 3)

    own = col * Z + dep

    g_dep = {}
    x_dep = {}
    g_col = []
    x_col = []
    for off in range(1, Z):
        g_dep[off] = send("depth", off, cot_ref.at[peer("depth", off)], g_all.at[own],
                          g_s.at[off, 0], g_r.at[off, 0])
    for off in range(1, C):
        g_col.append(send("col", off, cot_ref.at[dep], g_all.at[own], g_s.at[0, off], g_r.at[0, off]))
    for off in range(1, Z):
        x_dep[off] = send("depth", off, tok_ref, x_all.at[own], x_s.at[off, 0], x_r.at[off, 0])
    for off in range(1, C):
        x_col.append(send("col", off, tok_ref, x_all.at[own], x_s.at[0, off], x_r.at[0, off]))
    g_all[own] = cot_ref[dep]
    x_all[own] = tok_ref[...]
    for off in range(1, Z):
        g_dep[off].wait_recv()
        at = col * Z + source("depth", off)
        for co in range(1, C):
            g_col.append(send("col", co, g_all.at[at], g_all.at[at], g_s.at[off, co], g_r.at[off, co]))
    for off in range(1, Z):
        x_dep[off].wait_recv()
        at = col * Z + source("depth", off)
        for co in range(1, C):
            x_col.append(send("col", co, x_all.at[at], x_all.at[at], x_s.at[off, co], x_r.at[off, co]))

    def assemble(blocks, whole):
        def pair(i, carry):
            both = jnp.concatenate(
                [blocks[2 * i].astype(F32), blocks[2 * i + 1].astype(F32)], axis=0
            )
            whole[pl.ds(pl.multiple_of(16 * i, 16), 16), :] = both.astype(BF16)
            return carry

        lax.fori_loop(0, C * Z // 2, pair, 0)

    for copy in g_col:
        copy.wait_recv()
    assemble(g_all, g_out)
    load_out.wait()
    n_half, n_hid = pre_part.shape[1], pre_part.shape[2]
    block_h = block_of(n_hid)
    back_row = []
    for d in range(Z):
        def back_step(j, carry, d=d):
            at = pl.ds(pl.multiple_of(d * n_hid + j * block_h, block_h), block_h)
            part = against(g_out[...], w_out_v[at, :])
            back_part[:, d, :, cols_at(j, block_h)] = part.reshape(R, n_half, block_h)
            return carry

        lax.fori_loop(0, n_hid // block_h, back_step, 0)
        for off in range(1, R):
            back_row.append(send("row", off, back_part.at[peer("row", off), d], back_recv.at[off - 1, d],
                                 br_s.at[off - 1, d], br_r.at[off - 1, d]))
    for copy in back_row:
        copy.wait_recv()

    def back_sum(d):
        total = back_part[row, d]
        for off in range(1, R):
            total = total + back_recv[off - 1, d]
        return total

    back_dep = []
    for off in range(1, Z):
        d = peer("depth", off)
        back_send[off] = back_sum(d).astype(BF16)
        back_dep.append(send("depth", off, back_send.at[off], back_depth.at[off], bd_s.at[off], bd_r.at[off]))

    for copy in x_col:
        copy.wait_recv()
    assemble(x_all, x_out)
    load_in.wait()
    block_p = block_of(n_hid, 256)

    def pre_step(j, carry):
        part = jnp.dot(x_out[...], w_in_v[:, cols_at(j, block_p)], preferred_element_type=F32)
        pre_part[:, :, cols_at(j, block_p)] = part.reshape(R, n_half, block_p)
        return carry

    lax.fori_loop(0, n_hid // block_p, pre_step, 0)
    pre_row = [
        send("row", off, pre_part.at[peer("row", off)], pre_recv.at[off - 1],
             pre_s.at[off - 1], pre_r.at[off - 1])
        for off in range(1, R)
    ]
    for copy in pre_row:
        copy.wait_recv()
    for copy in back_dep:
        copy.wait_recv()
    pre = pre_part[row] + b_ref[...]
    for off in range(1, R):
        pre = pre + pre_recv[off - 1]
    back = back_sum(dep)
    for off in range(1, Z):
        back = back + back_depth[off].astype(F32)
    act, slope = gelu_pair(pre)
    grad_all[row] = (back * slope).astype(BF16)
    act_all[dep, row] = act.astype(BF16)
    grad_row = [
        send("row", off, grad_all.at[row], grad_all.at[row], grad_s.at[off], grad_r.at[off])
        for off in range(1, R)
    ]
    act_dep = {
        off: send("depth", off, act_all.at[dep, row], act_all.at[dep, row],
                  act_s.at[off, 0], act_r.at[off, 0])
        for off in range(1, Z)
    }
    act_row = [
        send("row", off, act_all.at[dep, row], act_all.at[dep, row],
             act_s.at[0, off], act_r.at[0, off])
        for off in range(1, R)
    ]
    for copy in grad_row:
        copy.wait_recv()
    grad_out[...] = grad_all[...].reshape(R * n_half, n_hid)

    n_tok = dep_send.shape[2]
    chunk = col_send.shape[3]
    block_f = block_of(chunk)
    from_col = []
    for k in range(N_CHUNK):
        def in_step(j, carry, k=k):
            at = pl.ds(pl.multiple_of(k * chunk + j * block_f, block_f), block_f)
            part = against(grad_out[...], w_in_v[at, :])
            col_send[k, :, :, cols_at(j, block_f)] = part.astype(BF16).reshape(C, Z * n_tok, block_f)
            return carry

        lax.fori_loop(0, chunk // block_f, in_step, 0)
        from_col.append([
            send("col", off, col_send.at[k, peer("col", off)], col_recv.at[k, off],
                 col_s.at[k, off], col_r.at[k, off])
            for off in range(1, C)
        ])
    bias_out[...] = jnp.sum(grad_out[...].astype(F32), axis=0, keepdims=True)
    for off in range(1, Z):
        act_dep[off].wait_recv()
        at = source("depth", off)
        for ro in range(1, R):
            act_row.append(send("row", ro, act_all.at[at, row], act_all.at[at, row],
                                act_s.at[off, ro], act_r.at[off, ro]))
    from_dep = []
    for k in range(N_CHUNK):
        for copy in from_col[k]:
            copy.wait_recv()
        total = col_send[k, col].astype(F32)
        for off in range(1, C):
            total = total + col_recv[k, off].astype(F32)
        for d in range(Z):
            dep_send[k, d] = total[d * n_tok:(d + 1) * n_tok, :].astype(BF16)
        from_dep.append([
            send("depth", off, dep_send.at[k, peer("depth", off)], dep_recv.at[k, off],
                 dep_s.at[k, off], dep_r.at[k, off])
            for off in range(1, Z)
        ])
    for copy in act_row:
        copy.wait_recv()
    for d in range(Z):
        act_out[d] = act_all[d].reshape(R * n_half, n_hid)
    for k in range(N_CHUNK):
        for copy in from_dep[k]:
            copy.wait_recv()
        total = dep_send[k, dep].astype(F32)
        for off in range(1, Z):
            total = total + dep_recv[k, off].astype(F32)
        in_out[:, k * chunk:(k + 1) * chunk] = total.astype(BF16)
    for copy in pending:
        copy.wait_send()


def grad_kernel(left_ref, right_ref, out_ref):
    out_ref[...] = over_tokens(left_ref[...], right_ref[...]).astype(BF16)


def shards(R, C, Z, tokens, cotangent, w_in, b_in, w_out):
    t, n_feat = tokens.shape
    n_hid = w_in.shape[1]
    n_d = w_out.shape[1]
    T = C * Z * t
    half = T // R
    chunk = n_feat // N_CHUNK
    cot = cotangent.reshape(t, Z, n_d).transpose(1, 0, 2)
    bias = lax.dynamic_slice_in_dim(b_in, lax.axis_index("depth") * n_hid, n_hid, 0).reshape(1, n_hid)
    vmem = pl.BlockSpec(memory_space=pltpu.VMEM)
    hbm = pl.BlockSpec(memory_space=pl.ANY)
    dma = pltpu.SemaphoreType.DMA
    shape = jax.ShapeDtypeStruct
    every_x, quarter_g, grad, act, b_grad, input_grad = pl.pallas_call(
        functools.partial(exchange_kernel, R, C, Z),
        out_shape=(
            shape((T, n_feat), BF16),
            shape((T, n_d), BF16),
            shape((T, n_hid), BF16),
            shape((Z, T, n_hid), BF16),
            shape((1, n_hid), F32),
            shape((t, n_feat), BF16),
        ),
        in_specs=[vmem, vmem, hbm, vmem, hbm],
        out_specs=(vmem,) * 6,
        scratch_shapes=[
            pltpu.VMEM(w_in.shape, BF16),
            pltpu.VMEM(w_out.shape, BF16),
            pltpu.VMEM((C * Z, t, n_feat), BF16),
            pltpu.VMEM((C * Z, t, n_d), BF16),
            pltpu.VMEM((R, half, n_hid), F32),
            pltpu.VMEM((R - 1, half, n_hid), F32),
            pltpu.VMEM((R, Z, half, n_hid), F32),
            pltpu.VMEM((R - 1, Z, half, n_hid), F32),
            pltpu.VMEM((Z, half, n_hid), BF16),
            pltpu.VMEM((Z, half, n_hid), BF16),
            pltpu.VMEM((Z, R, half, n_hid), BF16),
            pltpu.VMEM((R, half, n_hid), BF16),
            pltpu.VMEM((N_CHUNK, C, Z * t, chunk), BF16),
            pltpu.VMEM((N_CHUNK, C, Z * t, chunk), BF16),
            pltpu.VMEM((N_CHUNK, Z, t, chunk), BF16),
            pltpu.VMEM((N_CHUNK, Z, t, chunk), BF16),
            dma((2,)),
            dma((Z, C)), dma((Z, C)), dma((Z, C)), dma((Z, C)),
            dma((R - 1,)), dma((R - 1,)),
            dma((R - 1, Z)), dma((R - 1, Z)),
            dma((Z,)), dma((Z,)),
            dma((Z, R)), dma((Z, R)),
            dma((R,)), dma((R,)),
            dma((N_CHUNK, C)), dma((N_CHUNK, C)),
            dma((N_CHUNK, Z)), dma((N_CHUNK, Z)),
        ],
        compiler_params=pltpu.CompilerParams(
            collective_id=0, has_side_effects=True, vmem_limit_bytes=62 * 1024 * 1024
        ),
        cost_estimate=pl.CostEstimate(
            flops=6 * T * n_feat * n_hid, bytes_accessed=4 * n_feat * n_hid, transcendentals=half * n_hid
        ),
        name="exchange",
    )(tokens, cot, w_in, bias, w_out)

    block_f = block_of(n_feat)
    w_in_grad = pl.pallas_call(
        grad_kernel,
        grid=(n_feat // block_f,),
        in_specs=[
            pl.BlockSpec((T, block_f), lambda i: (0, i)),
            pl.BlockSpec((T, n_hid), lambda i: (0, 0)),
        ],
        out_specs=pl.BlockSpec((block_f, n_hid), lambda i: (i, 0)),
        out_shape=shape((n_feat, n_hid), BF16),
        name="w_in_grad",
    )(every_x, grad)
    block_h = block_of(n_hid)
    per = n_hid // block_h
    w_out_grad = pl.pallas_call(
        grad_kernel,
        grid=(Z, per),
        in_specs=[
            pl.BlockSpec((None, T, block_h), lambda d, j: (d, 0, j)),
            pl.BlockSpec((T, n_d), lambda d, j: (0, 0)),
        ],
        out_specs=pl.BlockSpec((block_h, n_d), lambda d, j: (d * per + j, 0)),
        out_shape=shape((Z * n_hid, n_d), BF16),
        name="w_out_grad",
    )(act, quarter_g)
    return (input_grad, w_in_grad, b_grad.reshape(n_hid), w_out_grad)


def solution(mesh):
    sizes = (mesh.shape["row"], mesh.shape["col"], mesh.shape["depth"])
    return jax.shard_map(
        functools.partial(shards, *sizes),
        mesh=mesh,
        in_specs=(
            P(("col", "depth"), "row"),
            P(("col", "depth"), "row"),
            P("row", ("col", "depth")),
            P("col"),
            P("col", ("row", "depth")),
        ),
        out_specs=(
            P(("col", "depth"), "row"),
            P("row", ("col", "depth")),
            P(("col", "depth")),
            P("col", ("row", "depth")),
        ),
        check_vma=False,
    )
```

```python
import functools

import jax
import jax.numpy as jnp
from jax import lax
from jax.experimental import pallas as pl
from jax.experimental.pallas import tpu as pltpu
from jax.sharding import PartitionSpec as P

coef = 0.7978845608
MESH = pl.DeviceIdType.MESH
F32 = jnp.float32
BF16 = jnp.bfloat16


def gelu_pair(pre):
    inner = coef * (pre + 0.044715 * pre * pre * pre)
    tanh_v = jnp.tanh(inner)
    act = 0.5 * pre * (1.0 + tanh_v)
    slope = 0.5 * (1.0 + tanh_v) + 0.5 * pre * (1.0 - tanh_v * tanh_v) * coef * (
        1.0 + 0.134145 * pre * pre
    )
    return (act, slope)


def against(left, right):
    return lax.dot_general(left, right, (((1,), (1,)), ((), ())), preferred_element_type=F32)


def over_tokens(left, right):
    return lax.dot_general(left, right, (((0,), (0,)), ((), ())), preferred_element_type=F32)


def block_of(size, largest=512):
    for block in (512, 384, 256, 128):
        if block <= largest and size % block == 0:
            return block
    return size


def cols_at(i, block):
    return pl.ds(pl.multiple_of(i * block, block), block)


def exchange_kernel(
    R, C, Z,
    tok_ref, cot_ref, w_in_hbm, b_ref, w_out_hbm,
    x_out, g_out, grad_out, act_out, bias_out, *rest,
):
    parts_out, rest = rest[:C], rest[C:]
    (
    w_in_v, w_out_v, x_all, g_all, pre_part, pre_recv, back_part, back_recv,
    back_send, back_depth, act_all, grad_all, rolled,
    w_sem, x_s, x_r, g_s, g_r, pre_s, pre_r, br_s, br_r, bd_s, bd_r,
    act_s, act_r, grad_s, grad_r,
    ) = rest
    row, col, dep = lax.axis_index("row"), lax.axis_index("col"), lax.axis_index("depth")
    size = {"row": R, "col": C, "depth": Z}
    here = {"row": row, "col": col, "depth": dep}

    def peer(axis, off):
        return lax.rem(here[axis] + off, size[axis])

    def source(axis, off):
        return lax.rem(here[axis] + size[axis] - off, size[axis])

    pending = []

    def send(axis, off, src, dst, s, r):
        copy = pltpu.make_async_remote_copy(
            src_ref=src, dst_ref=dst, send_sem=s, recv_sem=r,
            device_id={axis: peer(axis, off)}, device_id_type=MESH,
        )
        copy.start()
        pending.append(copy)
        return copy

    load_out = pltpu.make_async_copy(w_out_hbm, w_out_v, w_sem.at[0])
    load_in = pltpu.make_async_copy(w_in_hbm, w_in_v, w_sem.at[1])
    load_out.start()
    load_in.start()

    barrier = pltpu.get_barrier_semaphore()
    for axis in ("row", "col", "depth"):
        for off in range(1, size[axis]):
            pl.semaphore_signal(
                barrier, inc=1, device_id={axis: peer(axis, off)}, device_id_type=MESH
            )
    pl.semaphore_wait(barrier, R + C + Z - 3)

    own = col * Z + dep

    g_dep = {}
    x_dep = {}
    g_col = []
    x_col = []
    for off in range(1, Z):
        g_dep[off] = send("depth", off, cot_ref.at[peer("depth", off)], g_all.at[own],
                          g_s.at[off, 0], g_r.at[off, 0])
    for off in range(1, C):
        g_col.append(send("col", off, cot_ref.at[dep], g_all.at[own], g_s.at[0, off], g_r.at[0, off]))
    for off in range(1, Z):
        x_dep[off] = send("depth", off, tok_ref, x_all.at[own], x_s.at[off, 0], x_r.at[off, 0])
    for off in range(1, C):
        x_col.append(send("col", off, tok_ref, x_all.at[own], x_s.at[0, off], x_r.at[0, off]))
    g_all[own] = cot_ref[dep]
    x_all[own] = tok_ref[...]
    for off in range(1, Z):
        g_dep[off].wait_recv()
        at = col * Z + source("depth", off)
        for co in range(1, C):
            g_col.append(send("col", co, g_all.at[at], g_all.at[at], g_s.at[off, co], g_r.at[off, co]))
    for off in range(1, Z):
        x_dep[off].wait_recv()
        at = col * Z + source("depth", off)
        for co in range(1, C):
            x_col.append(send("col", co, x_all.at[at], x_all.at[at], x_s.at[off, co], x_r.at[off, co]))

    def assemble(blocks, whole):
        def pair(i, carry):
            both = jnp.concatenate(
                [blocks[2 * i].astype(F32), blocks[2 * i + 1].astype(F32)], axis=0
            )
            whole[pl.ds(pl.multiple_of(16 * i, 16), 16), :] = both.astype(BF16)
            return carry

        lax.fori_loop(0, C * Z // 2, pair, 0)

    for copy in g_col:
        copy.wait_recv()
    assemble(g_all, g_out)
    load_out.wait()
    n_half, n_hid = pre_part.shape[1], pre_part.shape[2]
    block_h = block_of(n_hid)
    order = [*range(1, Z), 0]

    def back_part_of(off):
        d = peer("depth", off)

        def back_step(j, carry):
            at = pl.ds(pl.multiple_of(d * n_hid + j * block_h, block_h), block_h)
            part = against(g_out[...], w_out_v[at, :])
            back_part[:, off, :, cols_at(j, block_h)] = part.reshape(R, n_half, block_h)
            return carry

        lax.fori_loop(0, n_hid // block_h, back_step, 0)
        return [
            send("row", ro, back_part.at[peer("row", ro), off], back_recv.at[ro - 1, off],
                 br_s.at[ro - 1, off], br_r.at[ro - 1, off])
            for ro in range(1, R)
        ]

    def back_sum(off):
        total = back_part[row, off]
        for ro in range(1, R):
            total = total + back_recv[ro - 1, off]
        return total

    back_row = {}
    back_dep = []

    def back_on(off):
        for copy in back_row[off]:
            copy.wait_recv()
        if off:
            back_send[off] = back_sum(off).astype(BF16)
            back_dep.append(send("depth", off, back_send.at[off], back_depth.at[off],
                                 bd_s.at[off], bd_r.at[off]))

    for n, off in enumerate(order):
        back_row[off] = back_part_of(off)
        if n:
            back_on(order[n - 1])
    back_on(order[-1])

    for copy in x_col:
        copy.wait_recv()
    assemble(x_all, x_out)
    load_in.wait()
    block_p = block_of(n_hid, 256)

    def pre_step(j, carry):
        part = jnp.dot(x_out[...], w_in_v[:, cols_at(j, block_p)], preferred_element_type=F32)
        pre_part[:, :, cols_at(j, block_p)] = part.reshape(R, n_half, block_p)
        return carry

    lax.fori_loop(0, n_hid // block_p, pre_step, 0)
    pre_row = [
        send("row", off, pre_part.at[peer("row", off)], pre_recv.at[off - 1],
             pre_s.at[off - 1], pre_r.at[off - 1])
        for off in range(1, R)
    ]
    for copy in pre_row:
        copy.wait_recv()
    for copy in back_dep:
        copy.wait_recv()
    pre = pre_part[row] + b_ref[...]
    for off in range(1, R):
        pre = pre + pre_recv[off - 1]
    back = back_sum(0)
    for off in range(1, Z):
        back = back + back_depth[off].astype(F32)
    act, slope = gelu_pair(pre)
    grad_all[row] = (back * slope).astype(BF16)
    act_all[dep, row] = act.astype(BF16)
    grad_row = [
        send("row", off, grad_all.at[row], grad_all.at[row], grad_s.at[off], grad_r.at[off])
        for off in range(1, R)
    ]
    act_dep = {
        off: send("depth", off, act_all.at[dep, row], act_all.at[dep, row],
                  act_s.at[off, 0], act_r.at[off, 0])
        for off in range(1, Z)
    }
    act_row = [
        send("row", off, act_all.at[dep, row], act_all.at[dep, row],
             act_s.at[0, off], act_r.at[0, off])
        for off in range(1, R)
    ]
    for copy in grad_row:
        copy.wait_recv()
    grad_out[...] = grad_all[...].reshape(R * n_half, n_hid)

    n_feat = x_out.shape[1]
    n_tok = rolled.shape[0] // C
    for off in range(C):
        at = pl.ds(pl.multiple_of(peer("col", off) * n_tok, n_tok), n_tok)
        rolled[off * n_tok:(off + 1) * n_tok, :] = grad_out[at, :]
    block_f = block_of(n_feat)

    def in_step(j, carry):
        at = cols_at(j, block_f)
        part = against(rolled[...], w_in_v[at, :])
        for off in range(C):
            parts_out[off][:, at] = part[off * n_tok:(off + 1) * n_tok, :].astype(parts_out[off].dtype)
        return carry

    lax.fori_loop(0, n_feat // block_f, in_step, 0)
    bias_out[...] = jnp.sum(grad_out[...].astype(F32), axis=0, keepdims=True)
    for off in range(1, Z):
        act_dep[off].wait_recv()
        at = source("depth", off)
        for ro in range(1, R):
            act_row.append(send("row", ro, act_all.at[at, row], act_all.at[at, row],
                                act_s.at[off, ro], act_r.at[off, ro]))
    for copy in act_row:
        copy.wait_recv()
    for d in range(Z):
        act_out[d] = act_all[d].reshape(R * n_half, n_hid)
    for copy in pending:
        copy.wait_send()


def grad_kernel(left_ref, right_ref, out_ref):
    out_ref[...] = over_tokens(left_ref[...], right_ref[...]).astype(BF16)


def shards(R, C, Z, tokens, cotangent, w_in, b_in, w_out):
    t, n_feat = tokens.shape
    n_hid = w_in.shape[1]
    n_d = w_out.shape[1]
    T = C * Z * t
    half = T // R
    cot = cotangent.reshape(t, Z, n_d).transpose(1, 0, 2)
    bias = lax.dynamic_slice_in_dim(b_in, lax.axis_index("depth") * n_hid, n_hid, 0).reshape(1, n_hid)
    vmem = pl.BlockSpec(memory_space=pltpu.VMEM)
    hbm = pl.BlockSpec(memory_space=pl.ANY)
    dma = pltpu.SemaphoreType.DMA
    shape = jax.ShapeDtypeStruct
    every_x, quarter_g, grad, act, b_grad, *parts = pl.pallas_call(
        functools.partial(exchange_kernel, R, C, Z),
        out_shape=(
            shape((T, n_feat), BF16),
            shape((T, n_d), BF16),
            shape((T, n_hid), BF16),
            shape((Z, T, n_hid), BF16),
            shape((1, n_hid), F32),
            shape((Z * t, n_feat), F32),
        ) + (shape((Z * t, n_feat), BF16),) * (C - 1),
        in_specs=[vmem, vmem, hbm, vmem, hbm],
        out_specs=(vmem,) * (5 + C),
        scratch_shapes=[
            pltpu.VMEM(w_in.shape, BF16),
            pltpu.VMEM(w_out.shape, BF16),
            pltpu.VMEM((C * Z, t, n_feat), BF16),
            pltpu.VMEM((C * Z, t, n_d), BF16),
            pltpu.VMEM((R, half, n_hid), F32),
            pltpu.VMEM((R - 1, half, n_hid), F32),
            pltpu.VMEM((R, Z, half, n_hid), F32),
            pltpu.VMEM((R - 1, Z, half, n_hid), F32),
            pltpu.VMEM((Z, half, n_hid), BF16),
            pltpu.VMEM((Z, half, n_hid), BF16),
            pltpu.VMEM((Z, R, half, n_hid), BF16),
            pltpu.VMEM((R, half, n_hid), BF16),
            pltpu.VMEM((T, n_hid), BF16),
            dma((2,)),
            dma((Z, C)), dma((Z, C)), dma((Z, C)), dma((Z, C)),
            dma((R - 1,)), dma((R - 1,)),
            dma((R - 1, Z)), dma((R - 1, Z)),
            dma((Z,)), dma((Z,)),
            dma((Z, R)), dma((Z, R)),
            dma((R,)), dma((R,)),
        ],
        compiler_params=pltpu.CompilerParams(
            collective_id=0, has_side_effects=True, vmem_limit_bytes=62 * 1024 * 1024
        ),
        cost_estimate=pl.CostEstimate(
            flops=6 * T * n_feat * n_hid, bytes_accessed=4 * n_feat * n_hid, transcendentals=half * n_hid
        ),
        name="exchange",
    )(tokens, cot, w_in, bias, w_out)

    def shifted(value, axis, n, off):
        return lax.ppermute(value, axis, [(i, (i + off) % n) for i in range(n)])

    from_col = [shifted(parts[off], "col", C, off) for off in range(1, C)]
    cost = pl.CostEstimate(
        flops=2 * T * n_feat * n_hid, bytes_accessed=2 * n_feat * n_hid, transcendentals=0
    )
    block_f = block_of(n_feat)
    w_in_grad = pl.pallas_call(
        grad_kernel,
        grid=(n_feat // block_f,),
        in_specs=[
            pl.BlockSpec((T, block_f), lambda i: (0, i)),
            pl.BlockSpec((T, n_hid), lambda i: (0, 0)),
        ],
        out_specs=pl.BlockSpec((block_f, n_hid), lambda i: (i, 0)),
        out_shape=shape((n_feat, n_hid), BF16),
        cost_estimate=cost,
        name="w_in_grad",
    )(every_x, grad)
    total = parts[0]
    for value in from_col:
        total = total + value.astype(F32)
    act, total, w_in_grad = lax.optimization_barrier((act, total, w_in_grad))
    total = total.reshape(Z, t, n_feat)

    def for_depth(off):
        at = lax.rem(lax.axis_index("depth") + off, Z)
        return lax.dynamic_index_in_dim(total, at, 0, keepdims=False)

    from_dep = [shifted(for_depth(off).astype(BF16), "depth", Z, off) for off in range(1, Z)]
    block_h = block_of(n_hid)
    per = n_hid // block_h
    w_out_grad = pl.pallas_call(
        grad_kernel,
        grid=(Z, per),
        in_specs=[
            pl.BlockSpec((None, T, block_h), lambda d, j: (d, 0, j)),
            pl.BlockSpec((T, n_d), lambda d, j: (0, 0)),
        ],
        out_specs=pl.BlockSpec((block_h, n_d), lambda d, j: (d * per + j, 0)),
        out_shape=shape((Z * n_hid, n_d), BF16),
        cost_estimate=cost,
        name="w_out_grad",
    )(act, quarter_g)
    input_sum = for_depth(0)
    for value in from_dep:
        input_sum = input_sum + value.astype(F32)
    input_grad = input_sum.astype(BF16)
    return (input_grad, w_in_grad, b_grad.reshape(n_hid), w_out_grad)


def solution(mesh):
    sizes = (mesh.shape["row"], mesh.shape["col"], mesh.shape["depth"])
    return jax.shard_map(
        functools.partial(shards, *sizes),
        mesh=mesh,
        in_specs=(
            P(("col", "depth"), "row"),
            P(("col", "depth"), "row"),
            P("row", ("col", "depth")),
            P("col"),
            P("col", ("row", "depth")),
        ),
        out_specs=(
            P(("col", "depth"), "row"),
            P("row", ("col", "depth")),
            P(("col", "depth")),
            P("col", ("row", "depth")),
        ),
        check_vma=False,
    )
```

```python
import functools

import jax
import jax.numpy as jnp
from jax import lax
from jax.experimental import pallas as pl
from jax.experimental.pallas import tpu as pltpu
from jax.sharding import PartitionSpec as P

coef = 0.7978845608
MESH = pl.DeviceIdType.MESH
F32 = jnp.float32
BF16 = jnp.bfloat16


def gelu_pair(pre):
    inner = coef * (pre + 0.044715 * pre * pre * pre)
    tanh_v = jnp.tanh(inner)
    act = 0.5 * pre * (1.0 + tanh_v)
    slope = 0.5 * (1.0 + tanh_v) + 0.5 * pre * (1.0 - tanh_v * tanh_v) * coef * (
        1.0 + 0.134145 * pre * pre
    )
    return (act, slope)


def against(left, right):
    return lax.dot_general(left, right, (((1,), (1,)), ((), ())), preferred_element_type=F32)


def over_tokens(left, right):
    return lax.dot_general(left, right, (((0,), (0,)), ((), ())), preferred_element_type=F32)


def block_of(size, largest=512):
    for block in (512, 384, 256, 128):
        if block <= largest and size % block == 0:
            return block
    return size


def cols_at(i, block):
    return pl.ds(pl.multiple_of(i * block, block), block)


def exchange_kernel(
    R, C, Z,
    tok_ref, cot_ref, w_in_hbm, b_ref, w_out_hbm,
    x_out, g_out, grad_out, act_out, bias_out, *rest,
):
    parts_out, rest = rest[:C], rest[C:]
    (
    w_in_v, w_out_v, x_all, g_all, pre_part, pre_recv, back_part, back_recv,
    back_send, back_depth, act_all, grad_all, rolled,
    w_sem, x_s, x_r, g_s, g_r, pre_s, pre_r, br_s, br_r, bd_s, bd_r,
    act_s, act_r, grad_s, grad_r,
    ) = rest
    row, col, dep = lax.axis_index("row"), lax.axis_index("col"), lax.axis_index("depth")
    size = {"row": R, "col": C, "depth": Z}
    here = {"row": row, "col": col, "depth": dep}

    def peer(axis, off):
        return lax.rem(here[axis] + off, size[axis])

    def source(axis, off):
        return lax.rem(here[axis] + size[axis] - off, size[axis])

    pending = []

    def send(axis, off, src, dst, s, r):
        copy = pltpu.make_async_remote_copy(
            src_ref=src, dst_ref=dst, send_sem=s, recv_sem=r,
            device_id={axis: peer(axis, off)}, device_id_type=MESH,
        )
        copy.start()
        pending.append(copy)
        return copy

    load_out = pltpu.make_async_copy(w_out_hbm, w_out_v, w_sem.at[0])
    load_in = pltpu.make_async_copy(w_in_hbm, w_in_v, w_sem.at[1])
    load_out.start()
    load_in.start()

    barrier = pltpu.get_barrier_semaphore()
    for axis in ("row", "col", "depth"):
        for off in range(1, size[axis]):
            pl.semaphore_signal(
                barrier, inc=1, device_id={axis: peer(axis, off)}, device_id_type=MESH
            )
    pl.semaphore_wait(barrier, R + C + Z - 3)

    own = col * Z + dep

    g_dep = {}
    x_dep = {}
    g_col = []
    x_col = []
    for off in range(1, Z):
        g_dep[off] = send("depth", off, cot_ref.at[peer("depth", off)], g_all.at[own],
                          g_s.at[off, 0], g_r.at[off, 0])
    for off in range(1, C):
        g_col.append(send("col", off, cot_ref.at[dep], g_all.at[own], g_s.at[0, off], g_r.at[0, off]))
    for off in range(1, Z):
        x_dep[off] = send("depth", off, tok_ref, x_all.at[own], x_s.at[off, 0], x_r.at[off, 0])
    for off in range(1, C):
        x_col.append(send("col", off, tok_ref, x_all.at[own], x_s.at[0, off], x_r.at[0, off]))
    g_all[own] = cot_ref[dep]
    x_all[own] = tok_ref[...]
    for off in range(1, Z):
        g_dep[off].wait_recv()
        at = col * Z + source("depth", off)
        for co in range(1, C):
            g_col.append(send("col", co, g_all.at[at], g_all.at[at], g_s.at[off, co], g_r.at[off, co]))
    for off in range(1, Z):
        x_dep[off].wait_recv()
        at = col * Z + source("depth", off)
        for co in range(1, C):
            x_col.append(send("col", co, x_all.at[at], x_all.at[at], x_s.at[off, co], x_r.at[off, co]))

    def assemble(blocks, whole):
        def pair(i, carry):
            both = jnp.concatenate(
                [blocks[2 * i].astype(F32), blocks[2 * i + 1].astype(F32)], axis=0
            )
            whole[pl.ds(pl.multiple_of(16 * i, 16), 16), :] = both.astype(BF16)
            return carry

        lax.fori_loop(0, C * Z // 2, pair, 0)

    for copy in g_col:
        copy.wait_recv()
    assemble(g_all, g_out)
    load_out.wait()
    n_half, n_hid = pre_part.shape[1], pre_part.shape[2]
    block_h = block_of(n_hid)
    order = [*range(1, Z), 0]

    def back_part_of(off):
        d = peer("depth", off)

        def back_step(j, carry):
            at = pl.ds(pl.multiple_of(d * n_hid + j * block_h, block_h), block_h)
            part = against(g_out[...], w_out_v[at, :])
            back_part[:, off, :, cols_at(j, block_h)] = part.reshape(R, n_half, block_h)
            return carry

        lax.fori_loop(0, n_hid // block_h, back_step, 0)
        return [
            send("row", ro, back_part.at[peer("row", ro), off], back_recv.at[ro - 1, off],
                 br_s.at[ro - 1, off], br_r.at[ro - 1, off])
            for ro in range(1, R)
        ]

    def back_sum(off):
        total = back_part[row, off]
        for ro in range(1, R):
            total = total + back_recv[ro - 1, off]
        return total

    back_row = {}
    back_dep = []

    def back_on(off):
        for copy in back_row[off]:
            copy.wait_recv()
        if off:
            back_send[off] = back_sum(off).astype(BF16)
            back_dep.append(send("depth", off, back_send.at[off], back_depth.at[off],
                                 bd_s.at[off], bd_r.at[off]))

    for n, off in enumerate(order):
        back_row[off] = back_part_of(off)
        if n:
            back_on(order[n - 1])
    back_on(order[-1])

    for copy in x_col:
        copy.wait_recv()
    assemble(x_all, x_out)
    load_in.wait()
    block_p = block_of(n_hid, 256)

    def pre_step(j, carry):
        part = jnp.dot(x_out[...], w_in_v[:, cols_at(j, block_p)], preferred_element_type=F32)
        pre_part[:, :, cols_at(j, block_p)] = part.reshape(R, n_half, block_p)
        return carry

    lax.fori_loop(0, n_hid // block_p, pre_step, 0)
    pre_row = [
        send("row", off, pre_part.at[peer("row", off)], pre_recv.at[off - 1],
             pre_s.at[off - 1], pre_r.at[off - 1])
        for off in range(1, R)
    ]
    for copy in pre_row:
        copy.wait_recv()
    for copy in back_dep:
        copy.wait_recv()
    pre = pre_part[row] + b_ref[...]
    for off in range(1, R):
        pre = pre + pre_recv[off - 1]
    back = back_sum(0)
    for off in range(1, Z):
        back = back + back_depth[off].astype(F32)
    act, slope = gelu_pair(pre)
    grad_all[row] = (back * slope).astype(BF16)
    act_all[dep, row] = act.astype(BF16)
    grad_row = [
        send("row", off, grad_all.at[row], grad_all.at[row], grad_s.at[off], grad_r.at[off])
        for off in range(1, R)
    ]
    act_dep = {
        off: send("depth", off, act_all.at[dep, row], act_all.at[dep, row],
                  act_s.at[off, 0], act_r.at[off, 0])
        for off in range(1, Z)
    }
    act_row = [
        send("row", off, act_all.at[dep, row], act_all.at[dep, row],
             act_s.at[0, off], act_r.at[0, off])
        for off in range(1, R)
    ]
    for copy in grad_row:
        copy.wait_recv()
    grad_out[...] = grad_all[...].reshape(R * n_half, n_hid)

    n_feat = x_out.shape[1]
    n_tok = rolled.shape[0] // C
    for off in range(C):
        at = pl.ds(pl.multiple_of(peer("col", off) * n_tok, n_tok), n_tok)
        rolled[off * n_tok:(off + 1) * n_tok, :] = grad_out[at, :]
    block_f = block_of(n_feat)

    def in_step(j, carry):
        at = cols_at(j, block_f)
        part = against(rolled[...], w_in_v[at, :])
        for off in range(C):
            parts_out[off][:, at] = part[off * n_tok:(off + 1) * n_tok, :].astype(parts_out[off].dtype)
        return carry

    lax.fori_loop(0, n_feat // block_f, in_step, 0)
    bias_out[...] = jnp.sum(grad_out[...].astype(F32), axis=0, keepdims=True)
    for off in range(1, Z):
        act_dep[off].wait_recv()
        at = source("depth", off)
        for ro in range(1, R):
            act_row.append(send("row", ro, act_all.at[at, row], act_all.at[at, row],
                                act_s.at[off, ro], act_r.at[off, ro]))
    for copy in act_row:
        copy.wait_recv()
    for d in range(Z):
        act_out[d] = act_all[d].reshape(R * n_half, n_hid)
    for copy in pending:
        copy.wait_send()


def grad_kernel(left_ref, right_ref, *refs):
    out_ref = refs[-1]
    rows, cols = out_ref.shape
    tall, wide = block_of(rows, 256), block_of(cols, 256)
    for m in range(0, rows, tall):
        left = left_ref[:, m:m + tall].T
        for n in range(0, cols, wide):
            part = jnp.dot(left, right_ref[:, n:n + wide], preferred_element_type=F32)
            out_ref[m:m + tall, n:n + wide] = part.astype(BF16)


def shards(R, C, Z, tokens, cotangent, w_in, b_in, w_out):
    t, n_feat = tokens.shape
    n_hid = w_in.shape[1]
    n_d = w_out.shape[1]
    T = C * Z * t
    half = T // R
    cot = cotangent.reshape(t, Z, n_d).transpose(1, 0, 2)
    bias = lax.dynamic_slice_in_dim(b_in, lax.axis_index("depth") * n_hid, n_hid, 0).reshape(1, n_hid)
    vmem = pl.BlockSpec(memory_space=pltpu.VMEM)
    hbm = pl.BlockSpec(memory_space=pl.ANY)
    dma = pltpu.SemaphoreType.DMA
    shape = jax.ShapeDtypeStruct
    every_x, quarter_g, grad, act, b_grad, *parts = pl.pallas_call(
        functools.partial(exchange_kernel, R, C, Z),
        out_shape=(
            shape((T, n_feat), BF16),
            shape((T, n_d), BF16),
            shape((T, n_hid), BF16),
            shape((Z, T, n_hid), BF16),
            shape((1, n_hid), F32),
            shape((Z * t, n_feat), F32),
        ) + (shape((Z * t, n_feat), BF16),) * (C - 1),
        in_specs=[vmem, vmem, hbm, vmem, hbm],
        out_specs=(vmem,) * (5 + C),
        scratch_shapes=[
            pltpu.VMEM(w_in.shape, BF16),
            pltpu.VMEM(w_out.shape, BF16),
            pltpu.VMEM((C * Z, t, n_feat), BF16),
            pltpu.VMEM((C * Z, t, n_d), BF16),
            pltpu.VMEM((R, half, n_hid), F32),
            pltpu.VMEM((R - 1, half, n_hid), F32),
            pltpu.VMEM((R, Z, half, n_hid), F32),
            pltpu.VMEM((R - 1, Z, half, n_hid), F32),
            pltpu.VMEM((Z, half, n_hid), BF16),
            pltpu.VMEM((Z, half, n_hid), BF16),
            pltpu.VMEM((Z, R, half, n_hid), BF16),
            pltpu.VMEM((R, half, n_hid), BF16),
            pltpu.VMEM((T, n_hid), BF16),
            dma((2,)),
            dma((Z, C)), dma((Z, C)), dma((Z, C)), dma((Z, C)),
            dma((R - 1,)), dma((R - 1,)),
            dma((R - 1, Z)), dma((R - 1, Z)),
            dma((Z,)), dma((Z,)),
            dma((Z, R)), dma((Z, R)),
            dma((R,)), dma((R,)),
        ],
        compiler_params=pltpu.CompilerParams(
            collective_id=0, has_side_effects=True, vmem_limit_bytes=62 * 1024 * 1024
        ),
        cost_estimate=pl.CostEstimate(
            flops=6 * T * n_feat * n_hid, bytes_accessed=4 * n_feat * n_hid, transcendentals=half * n_hid
        ),
        name="exchange",
    )(tokens, cot, w_in, bias, w_out)

    def shifted(value, axis, n, off):
        return lax.ppermute(value, axis, [(i, (i + off) % n) for i in range(n)])

    from_col = [shifted(parts[off], "col", C, off) for off in range(1, C)]
    cost = pl.CostEstimate(
        flops=T * n_feat * n_hid, bytes_accessed=n_feat * n_hid, transcendentals=0
    )
    block_f = block_of(n_feat)
    w_in_grad = pl.pallas_call(
        grad_kernel,
        grid=(n_feat // block_f,),
        in_specs=[
            pl.BlockSpec((T, block_f), lambda i: (0, i)),
            pl.BlockSpec((T, n_hid), lambda i: (0, 0)),
        ],
        out_specs=pl.BlockSpec((block_f, n_hid), lambda i: (i, 0)),
        out_shape=shape((n_feat, n_hid), BF16),
        cost_estimate=cost,
        name="w_in_grad",
    )(every_x, grad)
    block_h = block_of(n_hid)
    per = n_hid // block_h
    w_out_shape = shape((Z * n_hid, n_d), BF16)

    def w_out_part(first, last, *held):
        return pl.pallas_call(
            grad_kernel,
            grid=(last - first, per),
            in_specs=[
                pl.BlockSpec((None, T, block_h), lambda d, j: (first + d, 0, j)),
                pl.BlockSpec((T, n_d), lambda d, j: (0, 0)),
            ] + [hbm] * len(held),
            out_specs=pl.BlockSpec((block_h, n_d), lambda d, j: ((first + d) * per + j, 0)),
            out_shape=w_out_shape,
            input_output_aliases={2: 0} if held else {},
            cost_estimate=cost,
            name="w_out_grad",
        )(act, quarter_g, *held)

    w_out_grad = w_out_part(0, Z // 2)
    *from_col, w_in_grad, w_out_grad = lax.optimization_barrier((*from_col, w_in_grad, w_out_grad))
    total = parts[0]
    for value in from_col:
        total = total + value.astype(F32)
    total, w_out_grad = lax.optimization_barrier((total, w_out_grad))
    total = total.reshape(Z, t, n_feat)

    def for_depth(off):
        at = lax.rem(lax.axis_index("depth") + off, Z)
        return lax.dynamic_index_in_dim(total, at, 0, keepdims=False)

    from_dep = [shifted(for_depth(off).astype(BF16), "depth", Z, off) for off in range(1, Z)]
    w_out_grad = w_out_part(Z // 2, Z, w_out_grad)
    input_sum = for_depth(0)
    for value in from_dep:
        input_sum = input_sum + value.astype(F32)
    input_grad = input_sum.astype(BF16)
    return (input_grad, w_in_grad, b_grad.reshape(n_hid), w_out_grad)


def solution(mesh):
    sizes = (mesh.shape["row"], mesh.shape["col"], mesh.shape["depth"])
    return jax.shard_map(
        functools.partial(shards, *sizes),
        mesh=mesh,
        in_specs=(
            P(("col", "depth"), "row"),
            P(("col", "depth"), "row"),
            P("row", ("col", "depth")),
            P("col"),
            P("col", ("row", "depth")),
        ),
        out_specs=(
            P(("col", "depth"), "row"),
            P("row", ("col", "depth")),
            P(("col", "depth")),
            P("col", ("row", "depth")),
        ),
        check_vma=False,
    )
```

```python
import functools

import jax
import jax.numpy as jnp
from jax import lax
from jax.experimental import pallas as pl
from jax.experimental.pallas import tpu as pltpu
from jax.sharding import PartitionSpec as P

coef = 0.7978845608
MESH = pl.DeviceIdType.MESH
F32 = jnp.float32
BF16 = jnp.bfloat16


def gelu_pair(pre):
    inner = coef * (pre + 0.044715 * pre * pre * pre)
    tanh_v = jnp.tanh(inner)
    act = 0.5 * pre * (1.0 + tanh_v)
    slope = 0.5 * (1.0 + tanh_v) + 0.5 * pre * (1.0 - tanh_v * tanh_v) * coef * (
        1.0 + 0.134145 * pre * pre
    )
    return (act, slope)


def against(left, right):
    return lax.dot_general(left, right, (((1,), (1,)), ((), ())), preferred_element_type=F32)


def over_tokens(left, right):
    return lax.dot_general(left, right, (((0,), (0,)), ((), ())), preferred_element_type=F32)


def block_of(size, largest=512):
    for block in (512, 384, 256, 128):
        if block <= largest and size % block == 0:
            return block
    return size


def cols_at(i, block):
    return pl.ds(pl.multiple_of(i * block, block), block)


def exchange_kernel(
    R, C, Z,
    tok_ref, cot_ref, w_in_hbm, b_ref, w_out_hbm,
    x_out, g_out, grad_out, act_out, bias_out, *rest,
):
    parts_out, rest = rest[:C], rest[C:]
    (
    w_in_v, w_out_v, x_all, g_all, pre_part, pre_recv, back_part, back_recv,
    back_send, back_depth, act_all, grad_all, rolled,
    w_sem, x_s, x_r, g_s, g_r, pre_s, pre_r, br_s, br_r, bd_s, bd_r,
    act_s, act_r, grad_s, grad_r,
    ) = rest
    row, col, dep = lax.axis_index("row"), lax.axis_index("col"), lax.axis_index("depth")
    size = {"row": R, "col": C, "depth": Z}
    here = {"row": row, "col": col, "depth": dep}

    def peer(axis, off):
        return lax.rem(here[axis] + off, size[axis])

    def source(axis, off):
        return lax.rem(here[axis] + size[axis] - off, size[axis])

    pending = []

    def send(axis, off, src, dst, s, r):
        copy = pltpu.make_async_remote_copy(
            src_ref=src, dst_ref=dst, send_sem=s, recv_sem=r,
            device_id={axis: peer(axis, off)}, device_id_type=MESH,
        )
        copy.start()
        pending.append(copy)
        return copy

    load_out = pltpu.make_async_copy(w_out_hbm, w_out_v, w_sem.at[0])
    load_in = pltpu.make_async_copy(w_in_hbm, w_in_v, w_sem.at[1])
    load_out.start()
    load_in.start()

    barrier = pltpu.get_barrier_semaphore()
    for axis in ("row", "col", "depth"):
        for off in range(1, size[axis]):
            pl.semaphore_signal(
                barrier, inc=1, device_id={axis: peer(axis, off)}, device_id_type=MESH
            )
    pl.semaphore_wait(barrier, R + C + Z - 3)

    own = col * Z + dep

    g_dep = {}
    x_dep = {}
    g_col = []
    x_col = []
    for off in range(1, Z):
        g_dep[off] = send("depth", off, cot_ref.at[peer("depth", off)], g_all.at[own],
                          g_s.at[off, 0], g_r.at[off, 0])
    for off in range(1, C):
        g_col.append(send("col", off, cot_ref.at[dep], g_all.at[own], g_s.at[0, off], g_r.at[0, off]))
    for off in range(1, Z):
        x_dep[off] = send("depth", off, tok_ref, x_all.at[own], x_s.at[off, 0], x_r.at[off, 0])
    for off in range(1, C):
        x_col.append(send("col", off, tok_ref, x_all.at[own], x_s.at[0, off], x_r.at[0, off]))
    g_all[own] = cot_ref[dep]
    x_all[own] = tok_ref[...]
    for off in range(1, Z):
        g_dep[off].wait_recv()
        at = col * Z + source("depth", off)
        for co in range(1, C):
            g_col.append(send("col", co, g_all.at[at], g_all.at[at], g_s.at[off, co], g_r.at[off, co]))
    for off in range(1, Z):
        x_dep[off].wait_recv()
        at = col * Z + source("depth", off)
        for co in range(1, C):
            x_col.append(send("col", co, x_all.at[at], x_all.at[at], x_s.at[off, co], x_r.at[off, co]))

    def assemble(blocks, whole):
        def pair(i, carry):
            both = jnp.concatenate(
                [blocks[2 * i].astype(F32), blocks[2 * i + 1].astype(F32)], axis=0
            )
            whole[pl.ds(pl.multiple_of(16 * i, 16), 16), :] = both.astype(BF16)
            return carry

        lax.fori_loop(0, C * Z // 2, pair, 0)

    for copy in g_col:
        copy.wait_recv()
    assemble(g_all, g_out)
    load_out.wait()
    n_half, n_hid = pre_part.shape[1], pre_part.shape[2]
    block_h = block_of(n_hid)
    order = [*range(1, Z), 0]

    def back_part_of(off):
        d = peer("depth", off)

        def back_step(j, carry):
            at = pl.ds(pl.multiple_of(d * n_hid + j * block_h, block_h), block_h)
            part = against(g_out[...], w_out_v[at, :])
            back_part[:, off, :, cols_at(j, block_h)] = part.reshape(R, n_half, block_h)
            return carry

        lax.fori_loop(0, n_hid // block_h, back_step, 0)
        return [
            send("row", ro, back_part.at[peer("row", ro), off], back_recv.at[ro - 1, off],
                 br_s.at[ro - 1, off], br_r.at[ro - 1, off])
            for ro in range(1, R)
        ]

    def back_sum(off):
        total = back_part[row, off]
        for ro in range(1, R):
            total = total + back_recv[ro - 1, off]
        return total

    back_row = {}
    back_dep = []

    def back_on(off):
        for copy in back_row[off]:
            copy.wait_recv()
        if off:
            back_send[off] = back_sum(off).astype(BF16)
            back_dep.append(send("depth", off, back_send.at[off], back_depth.at[off],
                                 bd_s.at[off], bd_r.at[off]))

    for n, off in enumerate(order):
        back_row[off] = back_part_of(off)
        if n:
            back_on(order[n - 1])
    back_on(order[-1])

    for copy in x_col:
        copy.wait_recv()
    assemble(x_all, x_out)
    load_in.wait()
    block_p = block_of(n_hid, 256)

    def pre_step(j, carry):
        part = jnp.dot(x_out[...], w_in_v[:, cols_at(j, block_p)], preferred_element_type=F32)
        pre_part[:, :, cols_at(j, block_p)] = part.reshape(R, n_half, block_p)
        return carry

    lax.fori_loop(0, n_hid // block_p, pre_step, 0)
    pre_row = [
        send("row", off, pre_part.at[peer("row", off)], pre_recv.at[off - 1],
             pre_s.at[off - 1], pre_r.at[off - 1])
        for off in range(1, R)
    ]
    for copy in pre_row:
        copy.wait_recv()
    for copy in back_dep:
        copy.wait_recv()
    pre = pre_part[row] + b_ref[...]
    for off in range(1, R):
        pre = pre + pre_recv[off - 1]
    back = back_sum(0)
    for off in range(1, Z):
        back = back + back_depth[off].astype(F32)
    act, slope = gelu_pair(pre)
    grad_all[row] = (back * slope).astype(BF16)
    act_all[dep, row] = act.astype(BF16)
    grad_row = [
        send("row", off, grad_all.at[row], grad_all.at[row], grad_s.at[off], grad_r.at[off])
        for off in range(1, R)
    ]
    act_dep = {
        off: send("depth", off, act_all.at[dep, row], act_all.at[dep, row],
                  act_s.at[off, 0], act_r.at[off, 0])
        for off in range(1, Z)
    }
    act_row = [
        send("row", off, act_all.at[dep, row], act_all.at[dep, row],
             act_s.at[0, off], act_r.at[0, off])
        for off in range(1, R)
    ]
    for copy in grad_row:
        copy.wait_recv()
    grad_out[...] = grad_all[...].reshape(R * n_half, n_hid)

    n_feat = x_out.shape[1]
    n_tok = rolled.shape[0] // C
    for off in range(C):
        at = pl.ds(pl.multiple_of(peer("col", off) * n_tok, n_tok), n_tok)
        rolled[off * n_tok:(off + 1) * n_tok, :] = grad_out[at, :]
    block_f = block_of(n_feat)

    def in_step(j, carry):
        at = cols_at(j, block_f)
        part = against(rolled[...], w_in_v[at, :])
        for off in range(C):
            parts_out[off][:, at] = part[off * n_tok:(off + 1) * n_tok, :].astype(parts_out[off].dtype)
        return carry

    lax.fori_loop(0, n_feat // block_f, in_step, 0)
    bias_out[...] = jnp.sum(grad_out[...].astype(F32), axis=0, keepdims=True)
    for off in range(1, Z):
        act_dep[off].wait_recv()
        at = source("depth", off)
        for ro in range(1, R):
            act_row.append(send("row", ro, act_all.at[at, row], act_all.at[at, row],
                                act_s.at[off, ro], act_r.at[off, ro]))
    for copy in act_row:
        copy.wait_recv()
    for d in range(Z):
        act_out[d] = act_all[d].reshape(R * n_half, n_hid)
    for copy in pending:
        copy.wait_send()


def grad_kernel(first, n_parts, left_ref, right_ref, *refs):
    out_ref, held, sems = refs[-3:]
    n_left, cols = left_ref.shape[-1], right_ref.shape[-1]
    block = block_of(n_left)
    per = n_left // block
    tall, wide = block_of(block, 256), block_of(cols, 256)

    def copy_of(i):
        start = pl.multiple_of(i * block, block)
        return pltpu.make_async_copy(
            held.at[pl.ds(start, block), :],
            out_ref.at[pl.ds(pl.multiple_of(first * n_left + start, block), block), :],
            sems.at[i],
        )

    def make(i, carry):
        d, j = i // per, lax.rem(i, per)
        for m in range(0, block, tall):
            at = pl.ds(pl.multiple_of(j * block + m, tall), tall)
            left = left_ref[first + d, :, at].T
            rows = pl.ds(pl.multiple_of(i * block + m, tall), tall)
            for n in range(0, cols, wide):
                part = jnp.dot(left, right_ref[:, n:n + wide], preferred_element_type=F32)
                held[rows, n:n + wide] = part.astype(BF16)
        copy_of(i).start()
        return carry

    def finish(i, carry):
        copy_of(i).wait()
        return carry

    lax.fori_loop(0, n_parts * per, make, 0)
    lax.fori_loop(0, n_parts * per, finish, 0)


def shards(R, C, Z, tokens, cotangent, w_in, b_in, w_out):
    t, n_feat = tokens.shape
    n_hid = w_in.shape[1]
    n_d = w_out.shape[1]
    T = C * Z * t
    half = T // R
    cot = cotangent.reshape(t, Z, n_d).transpose(1, 0, 2)
    bias = lax.dynamic_slice_in_dim(b_in, lax.axis_index("depth") * n_hid, n_hid, 0).reshape(1, n_hid)
    vmem = pl.BlockSpec(memory_space=pltpu.VMEM)
    hbm = pl.BlockSpec(memory_space=pl.ANY)
    dma = pltpu.SemaphoreType.DMA
    shape = jax.ShapeDtypeStruct
    every_x, quarter_g, grad, act, b_grad, *parts = pl.pallas_call(
        functools.partial(exchange_kernel, R, C, Z),
        out_shape=(
            shape((T, n_feat), BF16),
            shape((T, n_d), BF16),
            shape((T, n_hid), BF16),
            shape((Z, T, n_hid), BF16),
            shape((1, n_hid), F32),
            shape((Z * t, n_feat), F32),
        ) + (shape((Z * t, n_feat), BF16),) * (C - 1),
        in_specs=[vmem, vmem, hbm, vmem, hbm],
        out_specs=(vmem,) * (5 + C),
        scratch_shapes=[
            pltpu.VMEM(w_in.shape, BF16),
            pltpu.VMEM(w_out.shape, BF16),
            pltpu.VMEM((C * Z, t, n_feat), BF16),
            pltpu.VMEM((C * Z, t, n_d), BF16),
            pltpu.VMEM((R, half, n_hid), F32),
            pltpu.VMEM((R - 1, half, n_hid), F32),
            pltpu.VMEM((R, Z, half, n_hid), F32),
            pltpu.VMEM((R - 1, Z, half, n_hid), F32),
            pltpu.VMEM((Z, half, n_hid), BF16),
            pltpu.VMEM((Z, half, n_hid), BF16),
            pltpu.VMEM((Z, R, half, n_hid), BF16),
            pltpu.VMEM((R, half, n_hid), BF16),
            pltpu.VMEM((T, n_hid), BF16),
            dma((2,)),
            dma((Z, C)), dma((Z, C)), dma((Z, C)), dma((Z, C)),
            dma((R - 1,)), dma((R - 1,)),
            dma((R - 1, Z)), dma((R - 1, Z)),
            dma((Z,)), dma((Z,)),
            dma((Z, R)), dma((Z, R)),
            dma((R,)), dma((R,)),
        ],
        compiler_params=pltpu.CompilerParams(
            collective_id=0, has_side_effects=True, vmem_limit_bytes=62 * 1024 * 1024
        ),
        cost_estimate=pl.CostEstimate(
            flops=6 * T * n_feat * n_hid, bytes_accessed=4 * n_feat * n_hid, transcendentals=half * n_hid
        ),
        name="exchange",
    )(tokens, cot, w_in, bias, w_out)

    def shifted(value, axis, n, off):
        return lax.ppermute(value, axis, [(i, (i + off) % n) for i in range(n)])

    from_col = [shifted(parts[off], "col", C, off) for off in range(1, C)]
    cost = pl.CostEstimate(
        flops=T * n_feat * n_hid, bytes_accessed=n_feat * n_hid, transcendentals=0
    )
    def weight_grad(left, right, first, last, name, *held):
        n_left = left.shape[-1]
        n_piece = (last - first) * (n_left // block_of(n_left))
        return pl.pallas_call(
            functools.partial(grad_kernel, first, last - first),
            in_specs=[vmem, vmem] + [hbm] * len(held),
            out_specs=hbm,
            out_shape=shape((left.shape[0] * n_left, right.shape[1]), BF16),
            scratch_shapes=[
                pltpu.VMEM(((last - first) * n_left, right.shape[1]), BF16),
                dma((n_piece,)),
            ],
            input_output_aliases={2: 0} if held else {},
            compiler_params=pltpu.CompilerParams(vmem_limit_bytes=40 * 1024 * 1024),
            cost_estimate=cost,
            name=name,
        )(left, right, *held)

    w_in_grad = weight_grad(every_x.reshape(1, T, n_feat), grad, 0, 1, "w_in_grad")
    w_out_grad = weight_grad(act, quarter_g, 0, Z // 2, "w_out_grad")
    *from_col, w_in_grad, w_out_grad = lax.optimization_barrier((*from_col, w_in_grad, w_out_grad))
    total = parts[0]
    for value in from_col:
        total = total + value.astype(F32)
    total, w_out_grad = lax.optimization_barrier((total, w_out_grad))
    total = total.reshape(Z, t, n_feat)

    def for_depth(off):
        at = lax.rem(lax.axis_index("depth") + off, Z)
        return lax.dynamic_index_in_dim(total, at, 0, keepdims=False)

    from_dep = [shifted(for_depth(off).astype(BF16), "depth", Z, off) for off in range(1, Z)]
    w_out_grad = weight_grad(act, quarter_g, Z // 2, Z, "w_out_grad", w_out_grad)
    input_sum = for_depth(0)
    for value in from_dep:
        input_sum = input_sum + value.astype(F32)
    input_grad = input_sum.astype(BF16)
    return (input_grad, w_in_grad, b_grad.reshape(n_hid), w_out_grad)


def solution(mesh):
    sizes = (mesh.shape["row"], mesh.shape["col"], mesh.shape["depth"])
    return jax.shard_map(
        functools.partial(shards, *sizes),
        mesh=mesh,
        in_specs=(
            P(("col", "depth"), "row"),
            P(("col", "depth"), "row"),
            P("row", ("col", "depth")),
            P("col"),
            P("col", ("row", "depth")),
        ),
        out_specs=(
            P(("col", "depth"), "row"),
            P("row", ("col", "depth")),
            P(("col", "depth")),
            P("col", ("row", "depth")),
        ),
        check_vma=False,
    )
```
